32 devices in a mesh: mp: 2 (over x), tok: 2 (over core), lat: 8 (over z, y).
Axes of the slice: x: 2, y: 2, z: 4, core: 2. Of those that a mesh axis runs over, the one named last changes fastest.
Arguments:
- inputs: bfloat16 [2, 384, 4608], P('mp', 'lat', 'tok'), may hold values from -6 to 6
- gate_w: bfloat16 [2, 4608, 18432], P('mp', 'tok', 'lat'), may hold values from -0.09375 to 0.09375
- up_w: bfloat16 [2, 4608, 18432], P('mp', 'tok', 'lat'), may hold values from -0.09375 to 0.09375
- down_w: bfloat16 [2, 18432, 4608], P('mp', 'lat', 'tok'), may hold values from -0.046875 to 0.046875
- enc_w: bfloat16 [2, 4608, 8192], P('mp', 'tok', 'lat'), may hold values from -0.0625 to 0.0625
- enc_bias: float32 [8192], P('lat'), may hold values from -3 to 3
- dec_w: bfloat16 [8192, 2, 4608], P('lat', 'mp', 'tok'), may hold values from -0.0625 to 0.0625
- dec_bias: float32 [2, 4608], P('mp', 'tok'), may hold values from -3 to 3
Outputs:
- recon_error: float32 [2, 384, 4608], P('mp', 'lat', 'tok')
- dec_grad: float32 [8192, 2, 4608], P('lat', 'mp', 'tok')
- latent_grad: float32 [384, 8192], P(None, 'lat')
The draws below stay inside these ranges and needn't reach their ends.
All inputs are finite; a program needn't handle non-finite values.
Results may differ from the reference program's by a relative error of at most 0.009.
Values may be sent and summed in bfloat16 or wider, within the bound.
No kernel may reach another device: no remote copies, remote signals or barrier semaphores. Data moves between devices by JAX's collectives and lax.ppermute only.
A program may use at most 128 MiB of HBM per device.

```python
import jax
import jax.numpy as jnp

D = 4608
FF = 18432
LAT = 8192
TOKENS = 384


def levels(own_key, extent, pieces, smallest, high):
    def one(dim, parts):
        steps = jax.random.uniform(jax.random.fold_in(jax.random.fold_in(own_key, 6), dim), (parts,), jnp.float32, smallest / len(pieces), high / len(pieces))
        return jnp.repeat(jnp.exp(steps), extent[dim] // parts).reshape((-1,) + (1,) * (len(extent) - dim - 1))

    gain = one(*pieces[0])
    for cut in pieces[1:]:
        gain = gain * one(*cut)
    return gain


def normal_values(stream_key, extent, spread, reach, cuts=(), dtype=jnp.bfloat16):
    drawn = spread * jax.random.normal(stream_key, extent, jnp.float32)
    if cuts:
        drawn = drawn * levels(stream_key, extent, cuts, -0.22, 0.18)
    return jnp.clip(drawn, -reach, reach).astype(dtype)


def setup_inputs(seed: int = 0) -> dict:
    seeds = jax.random.split(jax.random.key(seed), 9)
    return {
        "inputs": normal_values(seeds[0], (2, TOKENS, D), 1.0, 6.0, ((0, 2), (1, 8), (2, 2))),
        "gate_w": normal_values(seeds[1], (2, D, FF), D ** -0.5, 0.09375, ((0, 2), (1, 2), (2, 8))),
        "up_w": normal_values(seeds[2], (2, D, FF), D ** -0.5, 0.09375, ((0, 2), (1, 2), (2, 8))),
        "down_w": normal_values(seeds[3], (2, FF, D), FF ** -0.5, 0.046875, ((0, 2), (1, 8), (2, 2))),
        "enc_w": normal_values(seeds[4], (2, D, LAT), (2 * D) ** -0.5, 0.0625, ((0, 2), (1, 2), (2, 8))),
        "enc_bias": normal_values(seeds[5], (LAT,), 0.5, 3.0, ((0, 8),), jnp.float32),
        "dec_w": normal_values(seeds[6], (LAT, 2, D), LAT ** -0.5, 0.0625, ((0, 8), (1, 2), (2, 2))),
        "dec_bias": normal_values(seeds[7], (2, D), 0.5, 3.0, ((0, 2), (1, 2)), jnp.float32),
    }


def reference(inputs, gate_w, up_w, down_w, enc_w, enc_bias, dec_w, dec_bias):
    acts = []
    for model in range(2):
        x_full = inputs[model]
        gate = jnp.dot(x_full, gate_w[model], preferred_element_type=jnp.float32)
        up_sum = jnp.dot(x_full, up_w[model], preferred_element_type=jnp.float32)
        hidden = (jax.nn.gelu(gate, approximate=True) * up_sum).astype(jnp.bfloat16)
        acts.append(jnp.dot(hidden, down_w[model], preferred_element_type=jnp.float32).astype(jnp.bfloat16))
    pre = jnp.dot(acts[0], enc_w[0], preferred_element_type=jnp.float32) + jnp.dot(acts[1], enc_w[1], preferred_element_type=jnp.float32) + enc_bias
    codes = jnp.maximum(pre, 0.0).astype(jnp.bfloat16)
    errors = []
    grads = []
    latent_grad = jnp.zeros((TOKENS, LAT), jnp.float32)
    for model in range(2):
        decoder = dec_w[:, model, :]
        recon = jnp.dot(codes, decoder, preferred_element_type=jnp.float32) + dec_bias[model]
        error = recon - acts[model].astype(jnp.float32)
        errors.append(error)
        error_b = error.astype(jnp.bfloat16)
        grads.append(jnp.dot(codes.T, error_b, preferred_element_type=jnp.float32))
        latent_grad = latent_grad + jnp.dot(error_b, decoder.T, preferred_element_type=jnp.float32)
    return jnp.stack(errors), jnp.stack(grads, axis=1), latent_grad
```

```python
import jax
import jax.numpy as jnp
from jax import lax
from jax.experimental import pallas as pl
from jax.experimental.pallas import tpu as pltpu
from jax.sharding import PartitionSpec as P

F32, BF16 = jnp.float32, jnp.bfloat16
HALVES = ((0, 3), (1, 2))
SWAP2 = [(0, 1), (1, 0)]


def dot(a, b):
    return jnp.dot(a, b, preferred_element_type=F32)


def contract_rows(left, right):
    return lax.dot_general(left, right, (((0,), (0,)), ((), ())), preferred_element_type=F32)


def contract_cols(left, right):
    return lax.dot_general(left, right, (((1,), (1,)), ((), ())), preferred_element_type=F32)


def swap(x, k):
    return lax.ppermute(x, "lat", [(i, i ^ k) for i in range(8)])


def gather(x):
    got = {0: x}
    for z in (3, 1, 2):
        got[z] = swap(x, 2 * z)
    other = {z: swap(got[z], 1) for z in (0, 1, 3, 2)}
    return [jnp.concatenate([b for z in half for b in (got[z], other[z])], axis=0) for half in HALVES]


def scatter_half(p, half, rows):
    terms = []
    for j in (1, 0):
        z = half[j]
        mine = p[2 * j * rows:(2 * j + 1) * rows]
        away = p[(2 * j + 1) * rows:(2 * j + 2) * rows].astype(BF16)
        s = mine + swap(away, 1).astype(F32)
        terms.append(s if z == 0 else swap(s.astype(BF16), 2 * z).astype(F32))
    return terms


def pair_sum(p, axis):
    b = p.astype(BF16)
    return b.astype(F32) + lax.ppermute(b, axis, SWAP2).astype(F32)


def half_sum(p, tok):
    h = p.shape[0] // 2
    lo, hi = p[:h], p[h:]
    mine = jnp.where(tok == 0, lo, hi)
    other = jnp.where(tok == 0, hi, lo)
    return mine + lax.ppermute(other.astype(BF16), "tok", SWAP2).astype(F32)


def join(h, tok):
    o = lax.ppermute(h, "tok", SWAP2)
    return jnp.concatenate([jnp.where(tok == 0, h, o), jnp.where(tok == 0, o, h)], axis=0)


def grad_kernel(c0, c1, e0, e1, out):
    n, w = c0.shape[1], e0.shape[1]
    cols = w // 128
    r = contract_rows(c0[...], e0[...]) + contract_rows(c1[...], e1[...])
    for c in range(cols):
        out[pl.ds(c, n, cols), :] = r[:, c * 128:(c + 1) * 128]


def decoder_grad(codes, errs):
    rows, n = codes[0].shape
    w = errs[0].shape[1]
    step = 128
    cspec = pl.BlockSpec((rows, step), lambda i: (0, i))
    espec = pl.BlockSpec((rows, w), lambda i: (0, 0))
    out = pl.pallas_call(
        grad_kernel,
        grid=(n // step,),
        in_specs=[cspec, cspec, espec, espec],
        out_specs=pl.BlockSpec((step * w // 128, 128), lambda i: (i, 0)),
        out_shape=jax.ShapeDtypeStruct((n * w // 128, 128), F32),
        compiler_params=pltpu.CompilerParams(vmem_limit_bytes=24 << 20),
        cost_estimate=pl.CostEstimate(flops=4 * rows * n * w, bytes_accessed=4 * n * w, transcendentals=0),
    )(*codes, *errs)
    return out.reshape(n, 1, w)


def body(inputs, gate_w, up_w, down_w, enc_w, enc_bias, dec_w, dec_bias):
    me = lax.axis_index("lat")
    tok = lax.axis_index("tok")
    gate_l, up_l, down_l, enc_l = gate_w[0], up_w[0], down_w[0], enc_w[0]
    dec_l = dec_w[:, 0, :]
    rows = inputs.shape[1]
    terms = []
    for xa, half in zip(gather(inputs[0]), HALVES):
        g = half_sum(dot(xa, gate_l), tok)
        u = half_sum(dot(xa, up_l), tok)
        hid = join((jax.nn.gelu(g, approximate=True) * u).astype(BF16), tok)
        terms += scatter_half(dot(hid, down_l), half, rows)
    acts = sum(terms).astype(BF16)
    codes, terms = [], []
    for aa, half in zip(gather(acts), HALVES):
        pre = pair_sum(pair_sum(dot(aa, enc_l), "tok"), "mp")
        codes.append(jnp.maximum(pre + enc_bias, 0.0).astype(BF16))
        terms += scatter_half(dot(codes[-1], dec_l), half, rows)
    err = sum(terms) + dec_bias[0] - acts.astype(F32)
    errs = gather(err.astype(BF16))
    lat = {}
    for e, half in zip(errs, HALVES):
        l = pair_sum(pair_sum(contract_cols(e, dec_l), "tok"), "mp").reshape(2, 2, rows, -1)
        for j, z in enumerate(half):
            lat[z] = l[j]
    dec_grad = decoder_grad(codes, errs)
    la = jnp.stack([lat[z] for z in range(4)], axis=0).reshape(8, rows, -1)
    for bit in (1, 2, 4):
        sw = la.reshape(8 // (2 * bit), 2, bit, *la.shape[1:])[:, ::-1].reshape(la.shape)
        la = jnp.where((me & bit) != 0, sw, la)
    latent = la.reshape(8 * rows, -1)
    return (err[None], dec_grad, latent)


def plain_body(inputs, gate_w, up_w, down_w, enc_w, enc_bias, dec_w, dec_bias):
    x_rows = inputs[0]
    gathered = lax.all_gather(x_rows, "lat", axis=0, tiled=True)
    gate_local = gate_w[0]
    up_local = up_w[0]
    width = gate_local.shape[1]
    block = gathered
    both = lax.psum_scatter(
        jnp.concatenate(
            [
                jnp.dot(block, gate_local, preferred_element_type=jnp.float32),
                jnp.dot(block, up_local, preferred_element_type=jnp.float32),
            ],
            axis=1,
        ),
        "tok",
        scatter_dimension=0,
        tiled=True,
    )
    hidden = (jax.nn.gelu(both[:, :width], approximate=True) * both[:, width:]).astype(jnp.bfloat16)
    hidden_all = lax.all_gather(hidden, "tok", axis=0, tiled=True)
    down_local = down_w[0]
    block = hidden_all
    acts = lax.psum_scatter(
        jnp.dot(block, down_local, preferred_element_type=jnp.float32),
        "lat",
        scatter_dimension=0,
        tiled=True,
    ).astype(jnp.bfloat16)
    acts_all = lax.all_gather(acts, "lat", axis=0, tiled=True)
    partial_pre = jnp.dot(acts_all, enc_w[0], preferred_element_type=jnp.float32)
    pre = lax.psum(partial_pre, ("mp", "tok"))
    codes = jnp.maximum(pre + enc_bias, 0.0).astype(jnp.bfloat16)
    decoder = dec_w[:, 0, :]
    bias_row = dec_bias[0]
    block = codes
    recon = lax.psum_scatter(
        jnp.dot(block, decoder, preferred_element_type=jnp.float32),
        "lat",
        scatter_dimension=0,
        tiled=True,
    )
    error = recon + bias_row - acts.astype(jnp.float32)
    error_all = lax.all_gather(error.astype(jnp.bfloat16), "lat", axis=0, tiled=True)
    decoder_grad = contract_rows(codes, error_all)
    latent_grad = lax.psum(contract_cols(error_all, decoder), ("mp", "tok"))
    return (error[None], decoder_grad[:, None, :], latent_grad)


def solution(mesh):
    sizes = [mesh.shape[a] for a in ("mp", "tok", "lat")]
    step = body if sizes == [2, 2, 8] else plain_body
    in_specs = (
        P("mp", "lat", "tok"),
        P("mp", "tok", "lat"),
        P("mp", "tok", "lat"),
        P("mp", "lat", "tok"),
        P("mp", "tok", "lat"),
        P("lat"),
        P("lat", "mp", "tok"),
        P("mp", "tok"),
    )
    out_specs = (P("mp", "lat", "tok"), P("lat", "mp", "tok"), P(None, "lat"))
    return jax.shard_map(step, mesh=mesh, in_specs=in_specs, out_specs=out_specs, check_vma=False)
```

```python
import jax
import jax.numpy as jnp
from jax import lax
from jax.experimental import pallas as pl
from jax.experimental.pallas import tpu as pltpu
from jax.sharding import PartitionSpec as P

F32, BF16 = jnp.float32, jnp.bfloat16
SWAP2 = [(0, 1), (1, 0)]
LARGE = pl.CostEstimate(flops=20_000_000_000, bytes_accessed=1000, transcendentals=0)
MEDIUM = pl.CostEstimate(flops=1_200_000_000, bytes_accessed=1000, transcendentals=0)
SMALL = pl.CostEstimate(flops=1000, bytes_accessed=1000, transcendentals=0)


def contract_rows(left, right):
    return lax.dot_general(left, right, (((0,), (0,)), ((), ())), preferred_element_type=F32)


def contract_cols(left, right):
    return lax.dot_general(left, right, (((1,), (1,)), ((), ())), preferred_element_type=F32)


def dot(a, b):
    return jnp.dot(a, b, preferred_element_type=F32)


def after(x, *first):
    return lax.optimization_barrier((x,) + first)[0]


def swap(x, k):
    return lax.ppermute(x, "lat", [(i, i ^ k) for i in range(8)])


def pair(x, axis):
    return lax.ppermute(x, axis, SWAP2)


def gather(x, first=(), mid=(), weight=None):
    z1, y0, z3, z2 = swap(x, 2), swap(x, 1), swap(x, 6), swap(x, 4)
    y1 = swap(after(z1, y0), 1)
    y3 = swap(after(z3, *first), 1)
    if weight is not None:
        weight = load_after(weight, z3)
        mid = (weight,)
    y2 = swap(after(z2, *mid), 1)
    return (after(x, y1, z2), y0, z3, y3), (z1, y1, z2, y2), weight


def call(kernel, grid, in_specs, out_specs, out_shape, scratch=(), mib=24):
    return pl.pallas_call(
        kernel,
        grid=grid,
        in_specs=in_specs,
        out_specs=out_specs,
        out_shape=out_shape,
        scratch_shapes=scratch,
        compiler_params=pltpu.CompilerParams(vmem_limit_bytes=mib << 20),
        cost_estimate=LARGE,
    )


def whole(x):
    return pl.BlockSpec(x.shape, lambda i: (0,) * x.ndim)


def fast(shape, dtype):
    return pltpu.VMEM(tuple(shape), dtype)


def in_vmem(x):
    return pltpu.with_memory_space_constraint(x, pltpu.VMEM)


def vmem_call(kernel, args, out_shape, scratch=(), mib=8, cost=SMALL, scalar=None, first=()):
    spec = pl.BlockSpec(memory_space=pltpu.VMEM)
    n = len(out_shape) if isinstance(out_shape, (list, tuple)) else 0
    scalars = [] if scalar is None else [scalar]
    k = len(first)

    return pl.pallas_call(
        lambda *refs: kernel(*refs[k:]),
        in_specs=[pl.BlockSpec(memory_space=pl.ANY)] * k
        + [pl.BlockSpec(memory_space=pltpu.SMEM)] * len(scalars) + [spec] * len(args),
        out_specs=[spec] * n if n else spec,
        out_shape=out_shape,
        scratch_shapes=scratch,
        compiler_params=pltpu.CompilerParams(vmem_limit_bytes=mib << 20),
        cost_estimate=cost,
    )(*first, *scalars, *[in_vmem(a) for a in args])


def load_kernel(src, dst, sem):
    c = pltpu.make_async_copy(src, dst, sem)
    c.start()
    c.wait()


def load(w, *first):
    w = after(w, *first) if first else w
    return pl.pallas_call(
        load_kernel,
        in_specs=[pl.BlockSpec(memory_space=pltpu.HBM)],
        out_specs=pl.BlockSpec(memory_space=pltpu.VMEM),
        out_shape=fast(w.shape, w.dtype),
        scratch_shapes=[pltpu.SemaphoreType.DMA],
        compiler_params=pltpu.CompilerParams(vmem_limit_bytes=1 << 20),
        cost_estimate=SMALL,
    )(pltpu.with_memory_space_constraint(w, pltpu.HBM))


def load_after(w, first):
    def kernel(_, src, dst, sem):
        load_kernel(src, dst, sem)

    return pl.pallas_call(
        kernel,
        in_specs=[pl.BlockSpec(memory_space=pl.ANY), pl.BlockSpec(memory_space=pltpu.HBM)],
        out_specs=pl.BlockSpec(memory_space=pltpu.VMEM),
        out_shape=fast(w.shape, w.dtype),
        scratch_shapes=[pltpu.SemaphoreType.DMA],
        compiler_params=pltpu.CompilerParams(vmem_limit_bytes=1 << 20),
        cost_estimate=SMALL,
    )(first, pltpu.with_memory_space_constraint(w, pltpu.HBM))


def assemble(blocks, xs):
    r = blocks[0].shape[0]
    for k, b in enumerate(blocks):
        xs[k * r:(k + 1) * r, :] = b[...]


def tiles(n, w, step):
    w = next(k for k in (768, 512, w) if n % k == 0)

    def run(i, _):
        step(pl.ds(pl.multiple_of(i * w, w), w))
        return 0

    lax.fori_loop(0, n // w, run, 0)


def gate_up_kernel(b0, b1, b2, b3, gate, up, out, xs):
    assemble((b0, b1, b2, b3), xs)

    def step(cols):
        out[0, :, cols] = dot(xs[...], gate[:, cols]).astype(BF16)
        out[1, :, cols] = dot(xs[...], up[:, cols]).astype(BF16)

    tiles(gate.shape[1], 256, step)


def gate_up(blocks, gate, up):
    r, d = blocks[0].shape
    return vmem_call(gate_up_kernel, (*blocks, gate, up), fast((2, 4 * r, gate.shape[1]), BF16),
                     [pltpu.VMEM((4 * r, d), BF16)])


def store_parts(p, r, cols, keep, send0, send1):
    keep[0, :, cols] = p[:r]
    send0[:, cols] = p[r:2 * r].astype(BF16)
    keep[1, :, cols] = p[2 * r:3 * r]
    send1[:, cols] = p[3 * r:].astype(BF16)


def down_kernel(own, got, weight, keep, send0, send1, hid):
    def act(cols):
        v = own[:, :, cols].astype(F32) + got[:, :, cols].astype(F32)
        hid[:, cols] = (jax.nn.gelu(v[0], approximate=True) * v[1]).astype(BF16)

    tiles(hid.shape[1], 256, act)

    def step(cols):
        store_parts(dot(hid[...], weight[:, cols]), keep.shape[1], cols, keep, send0, send1)

    tiles(weight.shape[1], 256, step)


def parts_shapes(r, d):
    return [fast((2, r, d), F32)] + [fast((r, d), BF16)] * 2


def down(own, got, weight):
    _, m, n = own.shape
    return vmem_call(down_kernel, (own, got, weight), parts_shapes(m // 4, weight.shape[1]),
                     [pltpu.VMEM((m, n), BF16)])


def assemble_halves(tok, blocks, xs):
    r = blocks[0].shape[0]
    for k, b in enumerate(blocks):
        row = pl.multiple_of(((k // 2) ^ tok) * (2 * r) + (k % 2) * r, r)
        xs[pl.ds(row, r), :] = b[...]


def store_halves(p, cols, mine, away):
    h = mine.shape[0]
    mine[:, cols] = p[:h].astype(BF16)
    away[:, cols] = p[h:].astype(BF16)


def encode_kernel(tok, b0, b1, b2, b3, weight, mine, away, xs):
    assemble_halves(tok[0], (b0, b1, b2, b3), xs)

    def step(cols):
        store_halves(dot(xs[...], weight[:, cols]), cols, mine, away)

    tiles(weight.shape[1], 256, step)


def encode(tok, blocks, weight, cost=SMALL):
    r, d = blocks[0].shape
    return vmem_call(encode_kernel, (*blocks, weight), [fast((2 * r, weight.shape[1]), BF16)] * 2,
                     [pltpu.VMEM((4 * r, d), BF16)], cost=cost, scalar=tok)


def decode_kernel(tok, own0, got0, own1, got1, weight, codes0, codes1, *parts):
    h = own0.shape[0]
    for codes, own, got in ((codes0, own0, got0), (codes1, own1, got1)):
        codes[pl.ds(pl.multiple_of(tok[0] * h, h), h), :] = own[...]
        codes[pl.ds(pl.multiple_of((1 - tok[0]) * h, h), h), :] = got[...]

    def step(cols):
        w = weight[:, cols]
        for codes, out in ((codes0, parts[:3]), (codes1, parts[3:])):
            store_parts(dot(codes[...], w), h // 2, cols, *out)

    tiles(weight.shape[1], 256, step)


def decode(tok, own0, got0, own1, got1, weight):
    h, n = own0.shape
    return vmem_call(decode_kernel, (own0, got0, own1, got1, weight),
                     [fast((2 * h, n), BF16)] * 2 + parts_shapes(h // 2, weight.shape[1]) * 2, scalar=tok)


def latent_kernel(tok, b0, b1, b2, b3, weight, mine, away, xs):
    assemble_halves(tok[0], (b0, b1, b2, b3), xs)

    def step(cols):
        store_halves(contract_cols(xs[...], weight[cols, :]), cols, mine, away)

    tiles(weight.shape[0], 256, step)


def latent(tok, blocks, weight, cost=SMALL):
    r, d = blocks[0].shape
    return vmem_call(latent_kernel, (*blocks, weight), [fast((2 * r, weight.shape[0]), BF16)] * 2,
                     [pltpu.VMEM((4 * r, d), BF16)], cost=cost, scalar=tok)


def grid_assemble(blocks, xs):
    @pl.when(pl.program_id(0) == 0)
    def _():
        assemble(blocks, xs)


def grad_kernel(c0, c1, *refs):
    blocks, out, mark, es = refs[:8], refs[9], refs[10], refs[11]
    mark[...] = jnp.zeros_like(mark)
    grid_assemble(blocks, es)
    n, w = c0.shape[1], es.shape[1]
    m = c0.shape[0]
    cols = w // 128
    r = contract_rows(c0[...], es[:m]) + contract_rows(c1[...], es[m:])
    for c in range(cols):
        out[pl.ds(c, n, cols), :] = r[:, c * 128:(c + 1) * 128]


def decoder_grad(codes, blocks, first):
    m, n = codes[0].shape
    r, w = blocks[0].shape
    step = 256
    cspec = pl.BlockSpec((m, step), lambda i: (0, i))
    out, mark = call(
        grad_kernel, (n // step,),
        [cspec, cspec] + [whole(blocks[0])] * 8 + [pl.BlockSpec(memory_space=pl.ANY)],
        [pl.BlockSpec((step * w // 128, 128), lambda i: (i, 0)), pl.BlockSpec((8, 128), lambda i: (0, 0))],
        [jax.ShapeDtypeStruct((n * w // 128, 128), F32), jax.ShapeDtypeStruct((8, 128), F32)],
        [pltpu.VMEM((8 * r, w), BF16)],
    )(*codes, *blocks, first)
    return out.reshape(n, 1, w), mark


def order_kernel(who, a0, g0, a1, g1, out, sems):
    r = a0.shape[0] // 2
    for i in range(8):
        k = i ^ who[0]
        row = pl.multiple_of((k & 1) * r, r)
        second = (k >= 2) & (k < 6)
        mine = jnp.where(k >= 4, 1, 0) == who[1]
        for ref, here in ((a0, mine & ~second), (g0, ~mine & ~second), (a1, mine & second), (g1, ~mine & second)):
            @pl.when(here)
            def _():
                pltpu.make_async_copy(ref.at[pl.ds(row, r)], out.at[pl.ds(i * r, r)], sems.at[i]).start()
    for i in range(8):
        pltpu.make_async_copy(a0.at[pl.ds(0, r)], out.at[pl.ds(i * r, r)], sems.at[i]).wait()


def ordered(who, a0, g0, a1, g1):
    h, n = a0.shape
    spec = pl.BlockSpec(memory_space=pltpu.VMEM)
    return pl.pallas_call(
        order_kernel,
        in_specs=[pl.BlockSpec(memory_space=pltpu.SMEM)] + [spec] * 4,
        out_specs=pl.BlockSpec(memory_space=pl.ANY),
        out_shape=jax.ShapeDtypeStruct((4 * h, n), F32),
        scratch_shapes=[pltpu.SemaphoreType.DMA((8,))],
        compiler_params=pltpu.CompilerParams(vmem_limit_bytes=4 << 20),
        cost_estimate=SMALL,
    )(who, in_vmem(a0), in_vmem(g0), in_vmem(a1), in_vmem(g1))


def plus(mine, got):
    return mine + got.astype(F32)


def scatter(a, b):
    keep, send0, send3 = a
    got3 = swap(send3, 1)
    s3 = swap(plus(keep[1], got3).astype(BF16), 6)
    keep0, (keep, send1, send2) = keep[0], b
    got2 = swap(after(send2, got3), 1)
    got1 = swap(after(send1, got2), 1)
    s = plus(plus(keep0, swap(after(send0, got1), 1)), s3)
    t2 = plus(keep[1], got2).astype(BF16)
    s2 = swap(t2, 4)
    s1 = swap(plus(keep[0], after(got1, t2)).astype(BF16), 2)
    return plus(add(s, s2, MEDIUM), s1)


def add_kernel(a, b, out):
    out[...] = a[...].astype(F32) + b[...].astype(F32)


def add(a, b, cost=SMALL, first=()):
    return vmem_call(add_kernel, (a, b), fast(a.shape, F32), cost=cost, first=first)


def chip_sum(mine, away):
    return plus(mine.astype(F32), pair(away, "tok")).astype(BF16)


def code_kernel(q, m, bias, out):
    out[...] = jnp.maximum(q[...].astype(F32) + m[...].astype(F32) + bias[...], 0.0).astype(BF16)


def to_codes(q, bias):
    return vmem_call(code_kernel, (q, pair(q, "mp"), bias), fast(q.shape, BF16))


def body(inputs, gate_w, up_w, down_w, enc_w, enc_bias, dec_w, dec_bias):
    me = lax.axis_index("lat")
    tok = lax.axis_index("tok").reshape(1)
    gate_l, up_l, down_l, enc_l = gate_w[0], up_w[0], down_w[0], enc_w[0]
    dec_l = dec_w[:, 0, :]
    bias = enc_bias[None]
    gate_l = load(gate_l)
    up_l = load(up_l, gate_l)
    down_l = load(down_l, up_l)
    xa, xb, _ = gather(inputs[0], (up_l,), (down_l,))
    gl = after(gate_l, down_l)
    ga = gate_up(xa, gl, up_l)
    gb = gate_up((after(xb[0], ga),) + xb[1:], gate_l, up_l)
    pa = down(ga, pair(ga, "tok"), after(down_l, gb))
    pb = down(gb, pair(gb, "tok"), after(down_l, pa[0]))
    acts = scatter(pa, pb).astype(BF16)

    aa, ab, enc_2 = gather(acts, weight=enc_l)
    qa = chip_sum(*encode(tok, aa, enc_2))
    ha = to_codes(qa, bias)
    mine, away = encode(tok, (after(ab[0], qa),) + ab[1:], enc_2)
    halves = [ha, to_codes(chip_sum(after(mine, ha), away), bias)]
    joined = [c for h in halves for c in (h, pair(h, "tok"))]
    ca, cb, *r = decode(tok, *joined, dec_l)
    err = scatter(r[:3], r[3:]) + dec_bias[0] - acts.astype(F32)

    ea, eb, _ = gather(err.astype(BF16))
    dec_3 = load_after(dec_l, eb[2])
    mine, away = latent(tok, ea, dec_3)
    la = chip_sum(after(mine, eb[3]), away)
    lb = chip_sum(*latent(tok, (after(eb[0], la),) + eb[1:], dec_3))
    dec_grad, t = decoder_grad((ca, cb), ea + eb, lb)
    la, lb = [add(l, pair(l, "mp"), first=(t,)) for l in (la, lb)]
    who = jnp.concatenate([me.reshape(1), tok])
    lat = ordered(who, la, pair(la, "tok"), lb, pair(lb, "tok"))
    return (err[None], dec_grad, lat)


def plain_body(inputs, gate_w, up_w, down_w, enc_w, enc_bias, dec_w, dec_bias):
    x_rows = inputs[0]
    gathered = lax.all_gather(x_rows, "lat", axis=0, tiled=True)
    gate_local = gate_w[0]
    up_local = up_w[0]
    width = gate_local.shape[1]
    block = gathered
    both = lax.psum_scatter(
        jnp.concatenate(
            [
                jnp.dot(block, gate_local, preferred_element_type=jnp.float32),
                jnp.dot(block, up_local, preferred_element_type=jnp.float32),
            ],
            axis=1,
        ),
        "tok",
        scatter_dimension=0,
        tiled=True,
    )
    hidden = (jax.nn.gelu(both[:, :width], approximate=True) * both[:, width:]).astype(jnp.bfloat16)
    hidden_all = lax.all_gather(hidden, "tok", axis=0, tiled=True)
    down_local = down_w[0]
    block = hidden_all
    acts = lax.psum_scatter(
        jnp.dot(block, down_local, preferred_element_type=jnp.float32),
        "lat",
        scatter_dimension=0,
        tiled=True,
    ).astype(jnp.bfloat16)
    acts_all = lax.all_gather(acts, "lat", axis=0, tiled=True)
    partial_pre = jnp.dot(acts_all, enc_w[0], preferred_element_type=jnp.float32)
    pre = lax.psum(partial_pre, ("mp", "tok"))
    codes = jnp.maximum(pre + enc_bias, 0.0).astype(jnp.bfloat16)
    decoder = dec_w[:, 0, :]
    bias_row = dec_bias[0]
    block = codes
    recon = lax.psum_scatter(
        jnp.dot(block, decoder, preferred_element_type=jnp.float32),
        "lat",
        scatter_dimension=0,
        tiled=True,
    )
    error = recon + bias_row - acts.astype(jnp.float32)
    error_all = lax.all_gather(error.astype(jnp.bfloat16), "lat", axis=0, tiled=True)
    decoder_grad = contract_rows(codes, error_all)
    latent_grad = lax.psum(contract_cols(error_all, decoder), ("mp", "tok"))
    return (error[None], decoder_grad[:, None, :], latent_grad)


def solution(mesh):
    sizes = [mesh.shape[a] for a in ("mp", "tok", "lat")]
    step = body if sizes == [2, 2, 8] else plain_body
    in_specs = (
        P("mp", "lat", "tok"),
        P("mp", "tok", "lat"),
        P("mp", "tok", "lat"),
        P("mp", "lat", "tok"),
        P("mp", "tok", "lat"),
        P("lat"),
        P("lat", "mp", "tok"),
        P("mp", "tok"),
    )
    out_specs = (P("mp", "lat", "tok"), P("lat", "mp", "tok"), P(None, "lat"))
    return jax.shard_map(step, mesh=mesh, in_specs=in_specs, out_specs=out_specs, check_vma=False)
```

```python
import jax
import jax.numpy as jnp
from jax import lax
from jax.experimental import pallas as pl
from jax.experimental.pallas import tpu as pltpu
from jax.sharding import PartitionSpec as P

F32, BF16 = jnp.float32, jnp.bfloat16
SWAP2 = [(0, 1), (1, 0)]
LARGE = pl.CostEstimate(flops=20_000_000_000, bytes_accessed=1000, transcendentals=0)
MEDIUM = pl.CostEstimate(flops=1_200_000_000, bytes_accessed=1000, transcendentals=0)
SMALL = pl.CostEstimate(flops=1000, bytes_accessed=1000, transcendentals=0)


def contract_rows(left, right):
    return lax.dot_general(left, right, (((0,), (0,)), ((), ())), preferred_element_type=F32)


def contract_cols(left, right):
    return lax.dot_general(left, right, (((1,), (1,)), ((), ())), preferred_element_type=F32)


def dot(a, b):
    return jnp.dot(a, b, preferred_element_type=F32)


def after(x, *first):
    return lax.optimization_barrier((x,) + first)[0]


def swap(x, k):
    return lax.ppermute(x, "lat", [(i, i ^ k) for i in range(8)])


def pair(x, axis):
    return lax.ppermute(x, axis, SWAP2)


def gather(x, first=(), mid=()):
    z1, y0, z3, z2 = swap(x, 2), swap(x, 1), swap(x, 6), swap(x, 4)
    y1 = swap(after(z1, y0), 1)
    y3 = swap(after(z3, *first), 1)
    y2 = swap(after(z2, *mid), 1)
    return (after(x, y1, z2), y0, z3, y3), (z1, y1, z2, y2)


def gather_with(x, weight, work):
    z1, y0, z3, z2 = swap(x, 2), swap(x, 1), swap(x, 6), swap(x, 4)
    y1 = swap(after(z1, y0), 1)
    y3 = swap(z3, 1)
    weight = load_after(weight, z3)
    done = work((after(x, y1), y0, z3, y3), weight)
    y2 = swap(after(z2, done[0]), 1)
    return done, weight, (z1, y1, z2, y2), (x, y0, z3, y3)


def call(kernel, grid, in_specs, out_specs, out_shape, scratch=(), mib=24):
    return pl.pallas_call(
        kernel,
        grid=grid,
        in_specs=in_specs,
        out_specs=out_specs,
        out_shape=out_shape,
        scratch_shapes=scratch,
        compiler_params=pltpu.CompilerParams(vmem_limit_bytes=mib << 20),
        cost_estimate=LARGE,
    )


def whole(x):
    return pl.BlockSpec(x.shape, lambda i: (0,) * x.ndim)


def fast(shape, dtype):
    return pltpu.VMEM(tuple(shape), dtype)


def in_vmem(x):
    return pltpu.with_memory_space_constraint(x, pltpu.VMEM)


def vmem_call(kernel, args, out_shape, scratch=(), mib=8, cost=SMALL, scalar=None, first=()):
    spec = pl.BlockSpec(memory_space=pltpu.VMEM)
    n = len(out_shape) if isinstance(out_shape, (list, tuple)) else 0
    scalars = [] if scalar is None else [scalar]
    k = len(first)

    return pl.pallas_call(
        lambda *refs: kernel(*refs[k:]),
        in_specs=[pl.BlockSpec(memory_space=pl.ANY)] * k
        + [pl.BlockSpec(memory_space=pltpu.SMEM)] * len(scalars) + [spec] * len(args),
        out_specs=[spec] * n if n else spec,
        out_shape=out_shape,
        scratch_shapes=scratch,
        compiler_params=pltpu.CompilerParams(vmem_limit_bytes=mib << 20),
        cost_estimate=cost,
    )(*first, *scalars, *[in_vmem(a) for a in args])


def load_kernel(src, dst, sem):
    c = pltpu.make_async_copy(src, dst, sem)
    c.start()
    c.wait()


def load(w, *first):
    w = after(w, *first) if first else w
    return pl.pallas_call(
        load_kernel,
        in_specs=[pl.BlockSpec(memory_space=pltpu.HBM)],
        out_specs=pl.BlockSpec(memory_space=pltpu.VMEM),
        out_shape=fast(w.shape, w.dtype),
        scratch_shapes=[pltpu.SemaphoreType.DMA],
        compiler_params=pltpu.CompilerParams(vmem_limit_bytes=1 << 20),
        cost_estimate=SMALL,
    )(pltpu.with_memory_space_constraint(w, pltpu.HBM))


def load_after(w, first):
    def kernel(_, src, dst, sem):
        load_kernel(src, dst, sem)

    return pl.pallas_call(
        kernel,
        in_specs=[pl.BlockSpec(memory_space=pl.ANY), pl.BlockSpec(memory_space=pltpu.HBM)],
        out_specs=pl.BlockSpec(memory_space=pltpu.VMEM),
        out_shape=fast(w.shape, w.dtype),
        scratch_shapes=[pltpu.SemaphoreType.DMA],
        compiler_params=pltpu.CompilerParams(vmem_limit_bytes=1 << 20),
        cost_estimate=SMALL,
    )(first, pltpu.with_memory_space_constraint(w, pltpu.HBM))


def assemble(blocks, xs):
    r = blocks[0].shape[0]
    for k, b in enumerate(blocks):
        xs[k * r:(k + 1) * r, :] = b[...]


def tiles(n, w, step):
    w = next(k for k in (768, 512, w) if n % k == 0)

    def run(i, _):
        step(pl.ds(pl.multiple_of(i * w, w), w))
        return 0

    lax.fori_loop(0, n // w, run, 0)


def gate_up_kernel(b0, b1, b2, b3, gate, up, out, xs):
    assemble((b0, b1, b2, b3), xs)

    def step(cols):
        out[0, :, cols] = dot(xs[...], gate[:, cols]).astype(BF16)
        out[1, :, cols] = dot(xs[...], up[:, cols]).astype(BF16)

    tiles(gate.shape[1], 256, step)


def gate_up(blocks, gate, up):
    r, d = blocks[0].shape
    return vmem_call(gate_up_kernel, (*blocks, gate, up), fast((2, 4 * r, gate.shape[1]), BF16),
                     [pltpu.VMEM((4 * r, d), BF16)])


def store_parts(p, r, cols, keep, send0, send1):
    keep[0, :, cols] = p[:r]
    send0[:, cols] = p[r:2 * r].astype(BF16)
    keep[1, :, cols] = p[2 * r:3 * r]
    send1[:, cols] = p[3 * r:].astype(BF16)


def down_kernel(own, got, weight, keep, send0, send1, hid):
    def act(cols):
        v = own[:, :, cols].astype(F32) + got[:, :, cols].astype(F32)
        hid[:, cols] = (jax.nn.gelu(v[0], approximate=True) * v[1]).astype(BF16)

    tiles(hid.shape[1], 256, act)

    def step(cols):
        store_parts(dot(hid[...], weight[:, cols]), keep.shape[1], cols, keep, send0, send1)

    tiles(weight.shape[1], 256, step)


def parts_shapes(r, d):
    return [fast((2, r, d), F32)] + [fast((r, d), BF16)] * 2


def down(own, got, weight):
    _, m, n = own.shape
    return vmem_call(down_kernel, (own, got, weight), parts_shapes(m // 4, weight.shape[1]),
                     [pltpu.VMEM((m, n), BF16)])


def assemble_halves(tok, blocks, xs):
    r = blocks[0].shape[0]
    for k, b in enumerate(blocks):
        row = pl.multiple_of(((k // 2) ^ tok) * (2 * r) + (k % 2) * r, r)
        xs[pl.ds(row, r), :] = b[...]


def store_halves(p, cols, mine, away):
    h = mine.shape[0]
    mine[:, cols] = p[:h].astype(BF16)
    away[:, cols] = p[h:].astype(BF16)


def encode_kernel(tok, b0, b1, b2, b3, weight, mine, away, xs):
    assemble_halves(tok[0], (b0, b1, b2, b3), xs)

    def step(cols):
        store_halves(dot(xs[...], weight[:, cols]), cols, mine, away)

    tiles(weight.shape[1], 256, step)


def encode(tok, blocks, weight, cost=SMALL):
    r, d = blocks[0].shape
    return vmem_call(encode_kernel, (*blocks, weight), [fast((2 * r, weight.shape[1]), BF16)] * 2,
                     [pltpu.VMEM((4 * r, d), BF16)], cost=cost, scalar=tok)


def decode_kernel(tok, own0, got0, own1, got1, weight, codes0, codes1, *parts):
    h = own0.shape[0]
    for codes, own, got in ((codes0, own0, got0), (codes1, own1, got1)):
        codes[pl.ds(pl.multiple_of(tok[0] * h, h), h), :] = own[...]
        codes[pl.ds(pl.multiple_of((1 - tok[0]) * h, h), h), :] = got[...]

    def step(cols):
        w = weight[:, cols]
        for codes, out in ((codes0, parts[:3]), (codes1, parts[3:])):
            store_parts(dot(codes[...], w), h // 2, cols, *out)

    tiles(weight.shape[1], 256, step)


def decode(tok, own0, got0, own1, got1, weight):
    h, n = own0.shape
    return vmem_call(decode_kernel, (own0, got0, own1, got1, weight),
                     [fast((2 * h, n), BF16)] * 2 + parts_shapes(h // 2, weight.shape[1]) * 2, scalar=tok)


def latent_kernel(tok, b0, b1, b2, b3, weight, mine, away, xs):
    assemble_halves(tok[0], (b0, b1, b2, b3), xs)

    def step(cols):
        store_halves(contract_cols(xs[...], weight[cols, :]), cols, mine, away)

    tiles(weight.shape[0], 256, step)


def latent(tok, blocks, weight, cost=SMALL):
    r, d = blocks[0].shape
    return vmem_call(latent_kernel, (*blocks, weight), [fast((2 * r, weight.shape[0]), BF16)] * 2,
                     [pltpu.VMEM((4 * r, d), BF16)], cost=cost, scalar=tok)


def grid_assemble(blocks, xs):
    @pl.when(pl.program_id(0) == 0)
    def _():
        assemble(blocks, xs)


def grad_kernel(c0, c1, *refs):
    blocks, out, mark, es = refs[:8], refs[9], refs[10], refs[11]
    mark[...] = jnp.zeros_like(mark)
    grid_assemble(blocks, es)
    n, w = c0.shape[1], es.shape[1]
    m = c0.shape[0]
    cols = w // 128
    r = contract_rows(c0[...], es[:m]) + contract_rows(c1[...], es[m:])
    for c in range(cols):
        out[pl.ds(c, n, cols), :] = r[:, c * 128:(c + 1) * 128]


def decoder_grad(codes, blocks, first):
    m, n = codes[0].shape
    r, w = blocks[0].shape
    step = 256
    cspec = pl.BlockSpec((m, step), lambda i: (0, i))
    out, mark = call(
        grad_kernel, (n // step,),
        [cspec, cspec] + [whole(blocks[0])] * 8 + [pl.BlockSpec(memory_space=pl.ANY)],
        [pl.BlockSpec((step * w // 128, 128), lambda i: (i, 0)), pl.BlockSpec((8, 128), lambda i: (0, 0))],
        [jax.ShapeDtypeStruct((n * w // 128, 128), F32), jax.ShapeDtypeStruct((8, 128), F32)],
        [pltpu.VMEM((8 * r, w), BF16)],
    )(*codes, *blocks, first)
    return out.reshape(n, 1, w), mark


def order_kernel(who, a0, g0, a1, g1, out, sems):
    r = a0.shape[0] // 2
    for i in range(8):
        k = i ^ who[0]
        row = pl.multiple_of((k & 1) * r, r)
        second = (k >= 2) & (k < 6)
        mine = jnp.where(k >= 4, 1, 0) == who[1]
        for ref, here in ((a0, mine & ~second), (g0, ~mine & ~second), (a1, mine & second), (g1, ~mine & second)):
            @pl.when(here)
            def _():
                pltpu.make_async_copy(ref.at[pl.ds(row, r)], out.at[pl.ds(i * r, r)], sems.at[i]).start()
    for i in range(8):
        pltpu.make_async_copy(a0.at[pl.ds(0, r)], out.at[pl.ds(i * r, r)], sems.at[i]).wait()


def ordered(who, a0, g0, a1, g1):
    h, n = a0.shape
    spec = pl.BlockSpec(memory_space=pltpu.VMEM)
    return pl.pallas_call(
        order_kernel,
        in_specs=[pl.BlockSpec(memory_space=pltpu.SMEM)] + [spec] * 4,
        out_specs=pl.BlockSpec(memory_space=pl.ANY),
        out_shape=jax.ShapeDtypeStruct((4 * h, n), F32),
        scratch_shapes=[pltpu.SemaphoreType.DMA((8,))],
        compiler_params=pltpu.CompilerParams(vmem_limit_bytes=4 << 20),
        cost_estimate=SMALL,
    )(who, in_vmem(a0), in_vmem(g0), in_vmem(a1), in_vmem(g1))


def plus(mine, got):
    return mine + got.astype(F32)


def scatter(a, b):
    keep, send0, send3 = a
    got3 = swap(send3, 1)
    s3 = swap(plus(keep[1], got3).astype(BF16), 6)
    keep0, (keep, send1, send2) = keep[0], b
    got2 = swap(after(send2, got3), 1)
    got1 = swap(after(send1, got2), 1)
    s = plus(plus(keep0, swap(after(send0, got1), 1)), s3)
    t2 = plus(keep[1], got2).astype(BF16)
    s2 = swap(t2, 4)
    s1 = swap(plus(keep[0], after(got1, t2)).astype(BF16), 2)
    return plus(add(s, s2, MEDIUM), s1)


def add_kernel(a, b, out):
    out[...] = a[...].astype(F32) + b[...].astype(F32)


def add(a, b, cost=SMALL, first=()):
    return vmem_call(add_kernel, (a, b), fast(a.shape, F32), cost=cost, first=first)


def chip_sum(mine, away):
    return plus(mine.astype(F32), pair(away, "tok")).astype(BF16)


def code_kernel(q, m, bias, out):
    out[...] = jnp.maximum(q[...].astype(F32) + m[...].astype(F32) + bias[...], 0.0).astype(BF16)


def to_codes(q, bias):
    return vmem_call(code_kernel, (q, pair(q, "mp"), bias), fast(q.shape, BF16))


def body(inputs, gate_w, up_w, down_w, enc_w, enc_bias, dec_w, dec_bias):
    me = lax.axis_index("lat")
    tok = lax.axis_index("tok").reshape(1)
    gate_l, up_l, down_l, enc_l = gate_w[0], up_w[0], down_w[0], enc_w[0]
    dec_l = dec_w[:, 0, :]
    bias = enc_bias[None]
    gate_l = load(gate_l)
    up_l = load(up_l, gate_l)
    down_l = load(down_l, up_l)
    xa, xb = gather(inputs[0], (up_l,), (down_l,))
    gl = after(gate_l, down_l)
    ga = gate_up(xa, gl, up_l)
    gb = gate_up((after(xb[0], ga),) + xb[1:], gate_l, up_l)
    pa = down(ga, pair(ga, "tok"), after(down_l, gb))
    pb = down(gb, pair(gb, "tok"), after(down_l, pa[0]))
    acts = scatter(pa, pb).astype(BF16)

    ea, enc_2, ab, _ = gather_with(acts, enc_l, lambda b, w: encode(tok, b, w))
    qa = chip_sum(*ea)
    ha = to_codes(qa, bias)
    mine, away = encode(tok, (after(ab[0], qa),) + ab[1:], enc_2)
    halves = [ha, to_codes(chip_sum(after(mine, ha), away), bias)]
    joined = [c for h in halves for c in (h, pair(h, "tok"))]
    ca, cb, *r = decode(tok, *joined, dec_l)
    err = scatter(r[:3], r[3:]) + dec_bias[0] - acts.astype(F32)

    err_b = err.astype(BF16)
    lat_a, dec_3, eb, ea = gather_with(err_b, dec_l, lambda b, w: latent(tok, b, w))
    la = chip_sum(*lat_a)
    sa = add(la, pair(la, "mp"))
    mine, away = latent(tok, (after(eb[0], la),) + eb[1:], dec_3)
    lb = chip_sum(after(mine, sa), away)
    dec_grad, t = decoder_grad((ca, cb), ea + eb, lb)
    la, lb = sa, add(lb, pair(lb, "mp"), first=(t,))
    who = jnp.concatenate([me.reshape(1), tok])
    lat = ordered(who, la, pair(la, "tok"), lb, pair(lb, "tok"))
    return (err[None], dec_grad, lat)


def plain_body(inputs, gate_w, up_w, down_w, enc_w, enc_bias, dec_w, dec_bias):
    x_rows = inputs[0]
    gathered = lax.all_gather(x_rows, "lat", axis=0, tiled=True)
    gate_local = gate_w[0]
    up_local = up_w[0]
    width = gate_local.shape[1]
    block = gathered
    both = lax.psum_scatter(
        jnp.concatenate(
            [
                jnp.dot(block, gate_local, preferred_element_type=jnp.float32),
                jnp.dot(block, up_local, preferred_element_type=jnp.float32),
            ],
            axis=1,
        ),
        "tok",
        scatter_dimension=0,
        tiled=True,
    )
    hidden = (jax.nn.gelu(both[:, :width], approximate=True) * both[:, width:]).astype(jnp.bfloat16)
    hidden_all = lax.all_gather(hidden, "tok", axis=0, tiled=True)
    down_local = down_w[0]
    block = hidden_all
    acts = lax.psum_scatter(
        jnp.dot(block, down_local, preferred_element_type=jnp.float32),
        "lat",
        scatter_dimension=0,
        tiled=True,
    ).astype(jnp.bfloat16)
    acts_all = lax.all_gather(acts, "lat", axis=0, tiled=True)
    partial_pre = jnp.dot(acts_all, enc_w[0], preferred_element_type=jnp.float32)
    pre = lax.psum(partial_pre, ("mp", "tok"))
    codes = jnp.maximum(pre + enc_bias, 0.0).astype(jnp.bfloat16)
    decoder = dec_w[:, 0, :]
    bias_row = dec_bias[0]
    block = codes
    recon = lax.psum_scatter(
        jnp.dot(block, decoder, preferred_element_type=jnp.float32),
        "lat",
        scatter_dimension=0,
        tiled=True,
    )
    error = recon + bias_row - acts.astype(jnp.float32)
    error_all = lax.all_gather(error.astype(jnp.bfloat16), "lat", axis=0, tiled=True)
    decoder_grad = contract_rows(codes, error_all)
    latent_grad = lax.psum(contract_cols(error_all, decoder), ("mp", "tok"))
    return (error[None], decoder_grad[:, None, :], latent_grad)


def solution(mesh):
    sizes = [mesh.shape[a] for a in ("mp", "tok", "lat")]
    step = body if sizes == [2, 2, 8] else plain_body
    in_specs = (
        P("mp", "lat", "tok"),
        P("mp", "tok", "lat"),
        P("mp", "tok", "lat"),
        P("mp", "lat", "tok"),
        P("mp", "tok", "lat"),
        P("lat"),
        P("lat", "mp", "tok"),
        P("mp", "tok"),
    )
    out_specs = (P("mp", "lat", "tok"), P("lat", "mp", "tok"), P(None, "lat"))
    return jax.shard_map(step, mesh=mesh, in_specs=in_specs, out_specs=out_specs, check_vma=False)
```

```python
import jax
import jax.numpy as jnp
from jax import lax
from jax.experimental import pallas as pl
from jax.experimental.pallas import tpu as pltpu
from jax.sharding import PartitionSpec as P

F32, BF16 = jnp.float32, jnp.bfloat16
SWAP2 = [(0, 1), (1, 0)]
LARGE = pl.CostEstimate(flops=20_000_000_000, bytes_accessed=1000, transcendentals=0)
MEDIUM = pl.CostEstimate(flops=1_200_000_000, bytes_accessed=1000, transcendentals=0)
SMALL = pl.CostEstimate(flops=1000, bytes_accessed=1000, transcendentals=0)


def contract_rows(left, right):
    return lax.dot_general(left, right, (((0,), (0,)), ((), ())), preferred_element_type=F32)


def contract_cols(left, right):
    return lax.dot_general(left, right, (((1,), (1,)), ((), ())), preferred_element_type=F32)


def dot(a, b):
    return jnp.dot(a, b, preferred_element_type=F32)


def after(x, *first):
    return lax.optimization_barrier((x,) + first)[0]


def swap(x, k):
    return lax.ppermute(x, "lat", [(i, i ^ k) for i in range(8)])


def send_z(x, pairs):
    return lax.ppermute(x, "lat", [(2 * a + y, 2 * b + y) for a, b in pairs for y in range(2)])


def pair(x, axis):
    return lax.ppermute(x, axis, SWAP2)


def gather(x, first=(), mid=()):
    z1, y0, z3, z2 = swap(x, 2), swap(x, 1), swap(x, 6), swap(x, 4)
    y1 = swap(after(z1, y0), 1)
    y3 = swap(after(z3, *first), 1)
    y2 = swap(after(z2, *mid), 1)
    return (after(x, y1, z2), y0, z3, y3), (z1, y1, z2, y2)


def gather_with(x, weight, work):
    z1, y0, z3, z2 = swap(x, 2), swap(x, 1), swap(x, 6), swap(x, 4)
    y1 = swap(after(z1, y0), 1)
    y3 = swap(z3, 1)
    weight = load_after(weight, z3)
    done = work((after(x, y1), y0, z3, y3), weight)
    y2 = swap(after(z2, done[0]), 1)
    return done, weight, (z1, y1, z2, y2), (x, y0, z3, y3)


def call(kernel, grid, in_specs, out_specs, out_shape, scratch=(), mib=24):
    return pl.pallas_call(
        kernel,
        grid=grid,
        in_specs=in_specs,
        out_specs=out_specs,
        out_shape=out_shape,
        scratch_shapes=scratch,
        compiler_params=pltpu.CompilerParams(vmem_limit_bytes=mib << 20),
        cost_estimate=LARGE,
    )


def whole(x):
    return pl.BlockSpec(x.shape, lambda i: (0,) * x.ndim)


def fast(shape, dtype):
    return pltpu.VMEM(tuple(shape), dtype)


def in_vmem(x):
    return pltpu.with_memory_space_constraint(x, pltpu.VMEM)


def vmem_call(kernel, args, out_shape, scratch=(), mib=8, cost=SMALL, scalar=None, first=()):
    spec = pl.BlockSpec(memory_space=pltpu.VMEM)
    n = len(out_shape) if isinstance(out_shape, (list, tuple)) else 0
    scalars = [] if scalar is None else [scalar]
    k = len(first)

    return pl.pallas_call(
        lambda *refs: kernel(*refs[k:]),
        in_specs=[pl.BlockSpec(memory_space=pl.ANY)] * k
        + [pl.BlockSpec(memory_space=pltpu.SMEM)] * len(scalars) + [spec] * len(args),
        out_specs=[spec] * n if n else spec,
        out_shape=out_shape,
        scratch_shapes=scratch,
        compiler_params=pltpu.CompilerParams(vmem_limit_bytes=mib << 20),
        cost_estimate=cost,
    )(*first, *scalars, *[in_vmem(a) for a in args])


def load_kernel(src, dst, sem):
    c = pltpu.make_async_copy(src, dst, sem)
    c.start()
    c.wait()


def load(w, *first):
    w = after(w, *first) if first else w
    return pl.pallas_call(
        load_kernel,
        in_specs=[pl.BlockSpec(memory_space=pltpu.HBM)],
        out_specs=pl.BlockSpec(memory_space=pltpu.VMEM),
        out_shape=fast(w.shape, w.dtype),
        scratch_shapes=[pltpu.SemaphoreType.DMA],
        compiler_params=pltpu.CompilerParams(vmem_limit_bytes=1 << 20),
        cost_estimate=SMALL,
    )(pltpu.with_memory_space_constraint(w, pltpu.HBM))


def load_after(w, first):
    def kernel(_, src, dst, sem):
        load_kernel(src, dst, sem)

    return pl.pallas_call(
        kernel,
        in_specs=[pl.BlockSpec(memory_space=pl.ANY), pl.BlockSpec(memory_space=pltpu.HBM)],
        out_specs=pl.BlockSpec(memory_space=pltpu.VMEM),
        out_shape=fast(w.shape, w.dtype),
        scratch_shapes=[pltpu.SemaphoreType.DMA],
        compiler_params=pltpu.CompilerParams(vmem_limit_bytes=1 << 20),
        cost_estimate=SMALL,
    )(first, pltpu.with_memory_space_constraint(w, pltpu.HBM))


def assemble(blocks, xs):
    r = blocks[0].shape[0]
    for k, b in enumerate(blocks):
        xs[k * r:(k + 1) * r, :] = b[...]


def tiles(n, w, step):
    w = next(k for k in (768, 512, w) if n % k == 0)

    def run(i, _):
        step(pl.ds(pl.multiple_of(i * w, w), w))
        return 0

    lax.fori_loop(0, n // w, run, 0)


def gate_up_kernel(b0, b1, b2, b3, gate, up, out, xs):
    assemble((b0, b1, b2, b3), xs)

    def step(cols):
        out[0, :, cols] = dot(xs[...], gate[:, cols]).astype(BF16)
        out[1, :, cols] = dot(xs[...], up[:, cols]).astype(BF16)

    tiles(gate.shape[1], 256, step)


def gate_up(blocks, gate, up):
    r, d = blocks[0].shape
    return vmem_call(gate_up_kernel, (*blocks, gate, up), fast((2, 4 * r, gate.shape[1]), BF16),
                     [pltpu.VMEM((4 * r, d), BF16)])


def store_parts(p, r, cols, keep, send0, send1):
    keep[0, :, cols] = p[:r]
    send0[:, cols] = p[r:2 * r].astype(BF16)
    keep[1, :, cols] = p[2 * r:3 * r]
    send1[:, cols] = p[3 * r:].astype(BF16)


def down_kernel(own, got, weight, keep, send0, send1, hid):
    def act(cols):
        v = own[:, :, cols].astype(F32) + got[:, :, cols].astype(F32)
        hid[:, cols] = (jax.nn.gelu(v[0], approximate=True) * v[1]).astype(BF16)

    tiles(hid.shape[1], 256, act)

    def step(cols):
        store_parts(dot(hid[...], weight[:, cols]), keep.shape[1], cols, keep, send0, send1)

    tiles(weight.shape[1], 256, step)


def parts_shapes(r, d):
    return [fast((2, r, d), F32)] + [fast((r, d), BF16)] * 2


def down(own, got, weight):
    _, m, n = own.shape
    return vmem_call(down_kernel, (own, got, weight), parts_shapes(m // 4, weight.shape[1]),
                     [pltpu.VMEM((m, n), BF16)])


def assemble_halves(tok, blocks, xs):
    r = blocks[0].shape[0]
    for k, b in enumerate(blocks):
        row = pl.multiple_of(((k // 2) ^ tok) * (2 * r) + (k % 2) * r, r)
        xs[pl.ds(row, r), :] = b[...]


def store_halves(p, cols, mine, away):
    h = mine.shape[0]
    mine[:, cols] = p[:h].astype(BF16)
    away[:, cols] = p[h:].astype(BF16)


def encode_kernel(tok, b0, b1, b2, b3, weight, mine, away, xs):
    assemble_halves(tok[0], (b0, b1, b2, b3), xs)

    def step(cols):
        store_halves(dot(xs[...], weight[:, cols]), cols, mine, away)

    tiles(weight.shape[1], 256, step)


def encode(tok, blocks, weight, cost=SMALL):
    r, d = blocks[0].shape
    return vmem_call(encode_kernel, (*blocks, weight), [fast((2 * r, weight.shape[1]), BF16)] * 2,
                     [pltpu.VMEM((4 * r, d), BF16)], cost=cost, scalar=tok)


def decode_kernel(tok, own0, got0, own1, got1, weight, codes0, codes1, *parts):
    h = own0.shape[0]
    for codes, own, got in ((codes0, own0, got0), (codes1, own1, got1)):
        codes[pl.ds(pl.multiple_of(tok[0] * h, h), h), :] = own[...]
        codes[pl.ds(pl.multiple_of((1 - tok[0]) * h, h), h), :] = got[...]

    def step(cols):
        w = weight[:, cols]
        for codes, out in ((codes0, parts[:3]), (codes1, parts[3:])):
            store_parts(dot(codes[...], w), h // 2, cols, *out)

    tiles(weight.shape[1], 256, step)


def decode(tok, own0, got0, own1, got1, weight):
    h, n = own0.shape
    return vmem_call(decode_kernel, (own0, got0, own1, got1, weight),
                     [fast((2 * h, n), BF16)] * 2 + parts_shapes(h // 2, weight.shape[1]) * 2, scalar=tok)


def latent_kernel(tok, b0, b1, b2, b3, weight, mine, away, xs):
    assemble_halves(tok[0], (b0, b1, b2, b3), xs)

    def step(cols):
        store_halves(contract_cols(xs[...], weight[cols, :]), cols, mine, away)

    tiles(weight.shape[0], 256, step)


def latent(tok, blocks, weight, cost=SMALL):
    r, d = blocks[0].shape
    return vmem_call(latent_kernel, (*blocks, weight), [fast((2 * r, weight.shape[0]), BF16)] * 2,
                     [pltpu.VMEM((4 * r, d), BF16)], cost=cost, scalar=tok)


def grid_assemble(blocks, xs):
    @pl.when(pl.program_id(0) == 0)
    def _():
        assemble(blocks, xs)


def grad_kernel(c0, c1, *refs):
    blocks, out, mark, es = refs[:8], refs[9], refs[10], refs[11]
    mark[...] = jnp.zeros_like(mark)
    grid_assemble(blocks, es)
    n, w = c0.shape[1], es.shape[1]
    m = c0.shape[0]
    cols = w // 128
    r = contract_rows(c0[...], es[:m]) + contract_rows(c1[...], es[m:])
    for c in range(cols):
        out[pl.ds(c, n, cols), :] = r[:, c * 128:(c + 1) * 128]


def decoder_grad(codes, blocks, first):
    m, n = codes[0].shape
    r, w = blocks[0].shape
    step = 256
    cspec = pl.BlockSpec((m, step), lambda i: (0, i))
    out, mark = call(
        grad_kernel, (n // step,),
        [cspec, cspec] + [whole(blocks[0])] * 8 + [pl.BlockSpec(memory_space=pl.ANY)],
        [pl.BlockSpec((step * w // 128, 128), lambda i: (i, 0)), pl.BlockSpec((8, 128), lambda i: (0, 0))],
        [jax.ShapeDtypeStruct((n * w // 128, 128), F32), jax.ShapeDtypeStruct((8, 128), F32)],
        [pltpu.VMEM((8 * r, w), BF16)],
    )(*codes, *blocks, first)
    return out.reshape(n, 1, w), mark


def order_kernel(who, a0, g0, a1, g1, out, sems):
    r = a0.shape[0] // 2
    for i in range(8):
        k = i ^ who[0]
        row = pl.multiple_of((k & 1) * r, r)
        second = (k >= 2) & (k < 6)
        mine = jnp.where(k >= 4, 1, 0) == who[1]
        for ref, here in ((a0, mine & ~second), (g0, ~mine & ~second), (a1, mine & second), (g1, ~mine & second)):
            @pl.when(here)
            def _():
                pltpu.make_async_copy(ref.at[pl.ds(row, r)], out.at[pl.ds(i * r, r)], sems.at[i]).start()
    for i in range(8):
        pltpu.make_async_copy(a0.at[pl.ds(0, r)], out.at[pl.ds(i * r, r)], sems.at[i]).wait()


def ordered(who, a0, g0, a1, g1):
    h, n = a0.shape
    spec = pl.BlockSpec(memory_space=pltpu.VMEM)
    return pl.pallas_call(
        order_kernel,
        in_specs=[pl.BlockSpec(memory_space=pltpu.SMEM)] + [spec] * 4,
        out_specs=pl.BlockSpec(memory_space=pl.ANY),
        out_shape=jax.ShapeDtypeStruct((4 * h, n), F32),
        scratch_shapes=[pltpu.SemaphoreType.DMA((8,))],
        compiler_params=pltpu.CompilerParams(vmem_limit_bytes=4 << 20),
        cost_estimate=SMALL,
    )(who, in_vmem(a0), in_vmem(g0), in_vmem(a1), in_vmem(g1))


def plus(mine, got):
    return mine + got.astype(F32)


def scatter(a, b):
    keep, send0, send3 = a
    got3 = swap(send3, 1)
    t3 = plus(keep[1], got3).astype(BF16)
    inward, s3 = send_z(t3, ((0, 1), (3, 2))), send_z(t3, ((1, 2), (2, 1)))
    keep0, (keep, send1, send2) = keep[0], b
    got2 = swap(after(send2, got3), 1)
    got1 = swap(after(send1, got2), 1)
    s = plus(plus(keep0, swap(after(send0, got1), 1)), s3)
    t2 = plus(plus(keep[1], got2), inward).astype(BF16)
    s2 = swap(t2, 4)
    s1 = swap(plus(keep[0], after(got1, t2)).astype(BF16), 2)
    return plus(add(s, s2, MEDIUM), s1)


def add_kernel(a, b, out):
    out[...] = a[...].astype(F32) + b[...].astype(F32)


def add(a, b, cost=SMALL, first=()):
    return vmem_call(add_kernel, (a, b), fast(a.shape, F32), cost=cost, first=first)


def chip_sum(mine, away):
    return plus(mine.astype(F32), pair(away, "tok")).astype(BF16)


def code_kernel(q, m, bias, out):
    out[...] = jnp.maximum(q[...].astype(F32) + m[...].astype(F32) + bias[...], 0.0).astype(BF16)


def to_codes(q, bias):
    return vmem_call(code_kernel, (q, pair(q, "mp"), bias), fast(q.shape, BF16))


def body(inputs, gate_w, up_w, down_w, enc_w, enc_bias, dec_w, dec_bias):
    me = lax.axis_index("lat")
    tok = lax.axis_index("tok").reshape(1)
    gate_l, up_l, down_l, enc_l = gate_w[0], up_w[0], down_w[0], enc_w[0]
    dec_l = dec_w[:, 0, :]
    bias = enc_bias[None]
    gate_l = load(gate_l)
    up_l = load(up_l, gate_l)
    down_l = load(down_l, up_l)
    xa, xb = gather(inputs[0], (up_l,), (down_l,))
    gl = after(gate_l, down_l)
    ga = gate_up(xa, gl, up_l)
    gb = gate_up((after(xb[0], ga),) + xb[1:], gate_l, up_l)
    pa = down(ga, pair(ga, "tok"), after(down_l, gb))
    pb = down(gb, pair(gb, "tok"), after(down_l, pa[0]))
    acts = scatter(pa, pb).astype(BF16)

    ea, enc_2, ab, _ = gather_with(acts, enc_l, lambda b, w: encode(tok, b, w))
    qa = chip_sum(*ea)
    ha = to_codes(qa, bias)
    mine, away = encode(tok, (after(ab[0], qa),) + ab[1:], enc_2)
    halves = [ha, to_codes(chip_sum(after(mine, ha), away), bias)]
    joined = [c for h in halves for c in (h, pair(h, "tok"))]
    ca, cb, *r = decode(tok, *joined, dec_l)
    err = scatter(r[:3], r[3:]) + dec_bias[0] - acts.astype(F32)

    err_b = err.astype(BF16)
    lat_a, dec_3, eb, ea = gather_with(err_b, dec_l, lambda b, w: latent(tok, b, w))
    la = chip_sum(*lat_a)
    sa = add(la, pair(la, "mp"))
    mine, away = latent(tok, (after(eb[0], la),) + eb[1:], dec_3)
    lb = chip_sum(after(mine, sa), away)
    dec_grad, t = decoder_grad((ca, cb), ea + eb, lb)
    la, lb = sa, add(lb, pair(lb, "mp"), first=(t,))
    who = jnp.concatenate([me.reshape(1), tok])
    lat = ordered(who, la, pair(la, "tok"), lb, pair(lb, "tok"))
    return (err[None], dec_grad, lat)


def plain_body(inputs, gate_w, up_w, down_w, enc_w, enc_bias, dec_w, dec_bias):
    x_rows = inputs[0]
    gathered = lax.all_gather(x_rows, "lat", axis=0, tiled=True)
    gate_local = gate_w[0]
    up_local = up_w[0]
    width = gate_local.shape[1]
    block = gathered
    both = lax.psum_scatter(
        jnp.concatenate(
            [
                jnp.dot(block, gate_local, preferred_element_type=jnp.float32),
                jnp.dot(block, up_local, preferred_element_type=jnp.float32),
            ],
            axis=1,
        ),
        "tok",
        scatter_dimension=0,
        tiled=True,
    )
    hidden = (jax.nn.gelu(both[:, :width], approximate=True) * both[:, width:]).astype(jnp.bfloat16)
    hidden_all = lax.all_gather(hidden, "tok", axis=0, tiled=True)
    down_local = down_w[0]
    block = hidden_all
    acts = lax.psum_scatter(
        jnp.dot(block, down_local, preferred_element_type=jnp.float32),
        "lat",
        scatter_dimension=0,
        tiled=True,
    ).astype(jnp.bfloat16)
    acts_all = lax.all_gather(acts, "lat", axis=0, tiled=True)
    partial_pre = jnp.dot(acts_all, enc_w[0], preferred_element_type=jnp.float32)
    pre = lax.psum(partial_pre, ("mp", "tok"))
    codes = jnp.maximum(pre + enc_bias, 0.0).astype(jnp.bfloat16)
    decoder = dec_w[:, 0, :]
    bias_row = dec_bias[0]
    block = codes
    recon = lax.psum_scatter(
        jnp.dot(block, decoder, preferred_element_type=jnp.float32),
        "lat",
        scatter_dimension=0,
        tiled=True,
    )
    error = recon + bias_row - acts.astype(jnp.float32)
    error_all = lax.all_gather(error.astype(jnp.bfloat16), "lat", axis=0, tiled=True)
    decoder_grad = contract_rows(codes, error_all)
    latent_grad = lax.psum(contract_cols(error_all, decoder), ("mp", "tok"))
    return (error[None], decoder_grad[:, None, :], latent_grad)


def solution(mesh):
    sizes = [mesh.shape[a] for a in ("mp", "tok", "lat")]
    step = body if sizes == [2, 2, 8] else plain_body
    in_specs = (
        P("mp", "lat", "tok"),
        P("mp", "tok", "lat"),
        P("mp", "tok", "lat"),
        P("mp", "lat", "tok"),
        P("mp", "tok", "lat"),
        P("lat"),
        P("lat", "mp", "tok"),
        P("mp", "tok"),
    )
    out_specs = (P("mp", "lat", "tok"), P("lat", "mp", "tok"), P(None, "lat"))
    return jax.shard_map(step, mesh=mesh, in_specs=in_specs, out_specs=out_specs, check_vma=False)
```
